256 devices in a mesh: grp: 4 (over y), dev: 64 (over z, x, core).
Axes of the slice: x: 4, y: 4, z: 8, core: 2. Of those that a mesh axis runs over, the one named last changes fastest.
Arguments:
- ctrl_a: float32 [48, 32768], P(None, ('grp', 'dev')), parts along dimension 1, may hold values from -5 to 5
- ctrl_b: float32 [48, 32768], P(None, ('grp', 'dev')), parts along dimension 1, may hold values from -5 to 5
- pair_a: int32 [131072], P(('grp', 'dev')), parts along dimension 0, may hold values from 0 to 127
- pair_b_owner: int32 [131072, 1], P(('grp', 'dev')), parts along dimension 0, may hold values from 0 to 63; in each aligned block of 512 rows (0 to 511, 512 to 1023, ...) at most 16 rows name the same one
- pair_b_slot: int32 [131072], P(('grp', 'dev')), parts along dimension 0, may hold values from 0 to 127
- pair_count: int32 [256], P(('grp', 'dev')), parts along dimension 0, may hold values from 1 to 512, 16384 in all
Outputs:
- near_a: float32 [32768, 256], P(('grp', 'dev')), parts along dimension 0
- near_b: float32 [32768, 256], P(('grp', 'dev')), parts along dimension 0
The draws below stay inside these ranges and needn't reach their ends.
There are 4 independent parts, one for each index of `grp`. The reference program is written for one: setup_inputs(seed, part) draws one part's arguments, and reference() takes and returns one part's arrays. A program takes and returns all parts, laid end to end along the dimension named above; each array names one. Nothing has to cross between parts.
Inputs may be any that keep to these rules, and one draw needn't show every extreme that they name: `pair_b_owner`: among the 512 pair slots of one device, at most 16 name the same owner, a bound that some block reaches. `pair_count`: the counts of all devices sum to exactly 16384, and the largest is exactly 512.
All inputs are finite; a program needn't handle non-finite values.
Results may differ from the reference program's by a relative error of at most 0.00005.
Values sent between devices are 32-bit elements; how exact they have to be, the bound alone decides.
No kernel may reach another device: no remote copies, remote signals or barrier semaphores. Data moves between devices by JAX's collectives and lax.ppermute only.
A program may use at most 64 MiB of HBM per device.

```python
import math
import jax
import jax.numpy as jnp
import numpy as np
from jax import lax

PATCH_DEV = 128
PAIR_DEV = 512
SUB = 16
PATCHES = 8192
PAIRS = 32768
CAPB = 16
N_DEV = 64


def place_ends(array, key, smallest, top_value):
    shape = array.shape
    place = [jax.random.randint(jax.random.fold_in(key, axis), (), 0, shape[axis]) for axis in range(len(shape))]
    array = array.at[tuple(place)].set(smallest)
    longest = shape.index(max(shape))
    place[longest] = (place[longest] + 1) % shape[longest]
    return array.at[tuple(place)].set(top_value)


def shard_levels(stream_key, dims, pieces, least, largest):
    def one(position, blocks):
        heights = jax.random.uniform(jax.random.fold_in(jax.random.fold_in(stream_key, 6), position), (blocks,), jnp.float32, least / len(pieces), largest / len(pieces))
        return jnp.repeat(jnp.exp(heights), dims[position] // blocks).reshape((-1,) + (1,) * (len(dims) - position - 1))

    factor_of = one(*pieces[0])
    for cut in pieces[1:]:
        factor_of = factor_of * one(*cut)
    return factor_of


def length_profile(amount, total, limit, skew):
    portions = [(1 << 20) // math.isqrt(standing ** skew) + 1 for standing in range(2, amount + 1)]
    surplus, holding = total - limit - (amount - 1), [1] * (amount - 1)
    while surplus > 0:
        free = [i for i in range(amount - 1) if holding[i] < limit]
        pool, remaining = sum([portions[i] for i in free]), surplus
        for i in free:
            more = min(limit - holding[i], max(1, remaining * portions[i] // pool), surplus)
            holding[i] = holding[i] + more
            surplus = surplus - more
    return np.array([limit] + holding)


def ragged(own_key, number_of, total, reach, slope):
    if number_of == 2:
        one = jax.random.randint(own_key, (), max(1, total - reach), min(reach, total - 1) + 1)
        return jnp.stack([one, total - one])
    lengths = jnp.asarray(length_profile(number_of, total, reach, slope), jnp.int32)
    couples = (number_of - 1) // 2
    source_of, sink = lengths[1:1 + 2 * couples:2], lengths[2:2 + 2 * couples:2]
    slack = jnp.minimum(source_of - 1, reach - sink)
    shifted = jax.random.randint(jax.random.fold_in(own_key, 1), (couples,), 0, 1 << 20) % (slack + 1)
    lengths = lengths.at[1:1 + 2 * couples:2].set(source_of - shifted).at[2:2 + 2 * couples:2].set(sink + shifted)
    return lengths[jax.random.permutation(jax.random.fold_in(own_key, 2), number_of)]


def shared_out(key, own, number, rows, number_of, top, limit, lean):
    order = jax.random.permutation(key, number_of)
    crowded, common = shares(number_of, rows * top, limit, lean, True), shares(number_of, rows * top, limit, lean, False)
    places = jnp.arange(number_of)

    def named(lengths, turn):
        used = int((lengths > 0).sum())
        fixed = max(1, used // 4)
        moved = fixed + (places - fixed + turn * (used - fixed)) % max(1, number_of - fixed)
        return jnp.zeros((number_of,), jnp.int32).at[order[jnp.where(places < fixed, places, moved)]].set(jnp.asarray(lengths, jnp.int32))

    lengths = jnp.where(number % 4 == 0, named(crowded, number // 4), named(common, number - number // 4 - 1))
    mixed = jax.random.permutation(jax.random.fold_in(own, 3), number_of)
    source_of, taker = mixed[0:number_of // 2 * 2:2], mixed[1:number_of // 2 * 2:2]
    room = jnp.minimum(lengths[source_of] - 1, limit - lengths[taker]) // 2
    room = jnp.where((source_of == order[0]) | (taker == order[0]) | (lengths[taker] == 0), 0, jnp.maximum(room, 0))
    moved = jax.random.randint(jax.random.fold_in(own, 4), (number_of // 2,), 0, 1 << 20) % (room + 1)
    lengths = lengths.at[source_of].add(-moved).at[taker].add(moved)
    items = jnp.searchsorted(jnp.cumsum(lengths), jnp.arange(rows * top), side="right").astype(jnp.int32)
    table = items.reshape(top, rows).T
    table = table[jax.random.permutation(jax.random.fold_in(own, 1), rows)]
    turn = jax.random.randint(jax.random.fold_in(own, 2), (rows, 1), 0, top)
    return jnp.take_along_axis(table, (jnp.arange(top)[None, :] + turn) % top, axis=1)


def shares(amount, total, bound, lean, full):
    loads = [(1 << 20) // math.isqrt(rank ** lean) + 1 for rank in range(1, amount + 1)]
    largest = bound if full else min(bound, max(-(-total // amount), total * loads[0] // sum(loads)))
    least = 1 if total - largest >= amount - 1 else 0
    holding, surplus = [largest] + [least] * (amount - 1), total - largest - least * (amount - 1)
    while surplus > 0:
        candidates = [i for i in range(1, amount) if holding[i] < largest] or [i for i in range(1, amount) if holding[i] < bound]
        pool, remaining = sum([loads[i] for i in candidates]), surplus
        for i in candidates:
            more = min(bound - holding[i], max(1, remaining * loads[i] // pool), surplus)
            holding[i] = holding[i] + more
            surplus = surplus - more
    return np.array(holding)


def noise(stream_key, dims, scale, bound, split=(), held_as=jnp.bfloat16):
    array = scale * jax.random.normal(stream_key, dims, jnp.float32)
    if split:
        array = array * shard_levels(stream_key, dims, split, -0.22, 0.18)
    return jnp.clip(array, -bound, bound).astype(held_as)


def setup_inputs(seed: int = 0, part: int = 0) -> dict:
    key_of = jax.random.split(jax.random.key(seed), 7)
    part_splits = jax.random.split(jax.random.fold_in(key_of[6], part), 7)
    ctrl_a = noise(part_splits[0], (48, PATCHES), 1.0, 5.0, ((1, 64),), jnp.float32)
    ctrl_b = noise(part_splits[1], (48, PATCHES), 1.0, 5.0, ((1, 64),), jnp.float32)
    pair_a = place_ends(jax.random.randint(part_splits[2], (PAIRS,), 0, PATCH_DEV), jax.random.fold_in(part_splits[2], 1), 0, PATCH_DEV - 1).astype(jnp.int32)
    pair_b_owner_keys = jax.random.split(jax.random.fold_in(part_splits[3], 1), PAIRS // PAIR_DEV)
    pair_b_owner_turns = jax.random.permutation(jax.random.fold_in(part_splits[3], 3), PAIRS // PAIR_DEV)
    pair_b_owner = jax.vmap(lambda own, number: shared_out(jax.random.fold_in(part_splits[3], 2), own, number, PAIR_DEV, N_DEV, 1, CAPB, 2))(pair_b_owner_keys, pair_b_owner_turns).reshape((PAIRS, 1))
    pair_b_slot = place_ends(jax.random.randint(part_splits[4], (PAIRS,), 0, PATCH_DEV), jax.random.fold_in(part_splits[4], 1), 0, PATCH_DEV - 1).astype(jnp.int32)
    pair_count = ragged(part_splits[5], N_DEV, N_DEV * PAIR_DEV // 2, PAIR_DEV, 2).astype(jnp.int32)
    return {"ctrl_a": ctrl_a, "ctrl_b": ctrl_b, "pair_a": pair_a, "pair_b_owner": pair_b_owner, "pair_b_slot": pair_b_slot, "pair_count": pair_count}


CLIP_SQUARED = 4.0


def child_table():
    along = (jnp.arange(SUB, dtype=jnp.float32) + 0.5) / SUB
    other = 1.0 - along
    basis = jnp.stack([other ** 3, 3.0 * along * other ** 2, 3.0 * along ** 2 * other, along ** 3])
    table = basis[:, None, :, None] * basis[None, :, None, :]
    return table.reshape(16, SUB * SUB)


def evaluate(control, table):
    number = control.shape[1]
    return jnp.einsum("cis,ip->cps", control.reshape(3, 16, number), table, precision=lax.Precision.HIGHEST)


def pair_minima(control_a, control_b, table):
    points_a = evaluate(control_a, table).transpose(2, 0, 1)
    points_b = evaluate(control_b, table).transpose(2, 0, 1)

    def one_pair(item):
        near_side, far_side = item
        distance = (near_side[0][:, None] - far_side[0][None, :]) ** 2
        distance = distance + (near_side[1][:, None] - far_side[1][None, :]) ** 2
        distance = distance + (near_side[2][:, None] - far_side[2][None, :]) ** 2
        return jnp.min(distance, axis=1), jnp.min(distance, axis=0)

    row_minima, column_minima = lax.map(one_pair, (points_a, points_b), batch_size=16)
    return row_minima.T, column_minima.T


def reference(ctrl_a, ctrl_b, pair_a, pair_b_owner, pair_b_slot, pair_count):
    index = jnp.arange(PAIRS, dtype=jnp.int32)
    device = (index // PAIR_DEV).astype(jnp.int32)
    live = (index % PAIR_DEV) < jnp.take(pair_count, device)
    first_patch = (device * PATCH_DEV + pair_a).astype(jnp.int32)
    second_patch = (pair_b_owner[:, 0] * PATCH_DEV + pair_b_slot).astype(jnp.int32)
    control_a = jnp.take(ctrl_a, first_patch, axis=1)
    control_b = jnp.take(ctrl_b, second_patch, axis=1)
    row_minima, column_minima = pair_minima(control_a, control_b, child_table())
    row_minima = jnp.where(live[None, :], row_minima, CLIP_SQUARED)
    column_minima = jnp.where(live[None, :], column_minima, CLIP_SQUARED)
    near_a = jnp.minimum(jax.ops.segment_min(row_minima.T, first_patch, num_segments=PATCH_DEV * N_DEV), CLIP_SQUARED)
    near_b = jnp.minimum(jax.ops.segment_min(column_minima.T, second_patch, num_segments=PATCH_DEV * N_DEV), CLIP_SQUARED)
    return near_a, near_b
```

```python
import jax
import jax.numpy as jnp
import ml_dtypes
import numpy as np
from jax import lax
from jax.experimental import pallas as pl
from jax.experimental.pallas import tpu as pltpu
from jax.sharding import PartitionSpec as P

SUB = 16
CHILDREN = SUB * SUB
CLIP_SQUARED = 4.0
ROOM = 16
GROUP = 4
DEPTH = 32
VMEM_BYTES = 48 * 2**20
F32 = jnp.float32
BF16 = jnp.bfloat16
HIGHEST = lax.Precision.HIGHEST
IN_VMEM = pl.BlockSpec(memory_space=pltpu.VMEM)
IN_SMEM = pl.BlockSpec(memory_space=pltpu.SMEM)


def bernstein_table():
    along = (np.arange(SUB) + 0.5) / SUB
    other = 1.0 - along
    basis = np.stack([other**3, 3.0 * along * other**2, 3.0 * along**2 * other, along**3])
    return (basis[:, None, :, None] * basis[None, :, None, :]).reshape(16, CHILDREN)


def table_pieces():
    left = bernstein_table().T
    parts = []
    for _ in range(3):
        parts.append(left.astype(np.float32).astype(ml_dtypes.bfloat16))
        left = left - parts[-1].astype(np.float64)
    one, two, three = parts
    return np.concatenate([one, two, three, one, two, one], axis=1)


def pieces(x):
    one = x.astype(BF16)
    rest = x - one.astype(F32)
    two = rest.astype(BF16)
    return one, two, (rest - two.astype(F32)).astype(BF16)


def own_features_kernel(ctrl_ref, table_ref, features_ref, centre_ref, norm_ref):
    patches = ctrl_ref.shape[1]
    control = ctrl_ref[...].T
    table = table_ref[...]
    centred, centre = [], []
    norm = jnp.zeros((patches, CHILDREN), F32)
    for c in range(3):
        block = control[:, c * 16 : (c + 1) * 16]
        mean = jnp.sum(block, axis=1, keepdims=True) * (1.0 / 16.0)
        block = block - mean
        points = jnp.dot(block, table, precision=HIGHEST, preferred_element_type=F32)
        norm = norm + points * points
        centred.append(block)
        centre.append(mean)
    norm_ref[...] = norm
    coordinate = jnp.minimum(lax.broadcasted_iota(jnp.int32, (1, 128), 1) % DEPTH // 9, 2)
    centre_ref[...] = jnp.where(
        coordinate == 0, centre[0], jnp.where(coordinate == 1, centre[1], centre[2])
    )
    centred = jnp.concatenate(centred, axis=1)
    table = jnp.concatenate([table] * 3, axis=0)
    row = lax.broadcasted_iota(jnp.int32, (DEPTH, 48), 0)
    lane = lax.broadcasted_iota(jnp.int32, (DEPTH, 48), 1)
    own = (lane // 16 == jnp.minimum(row // 9, 2)).astype(F32)
    row = lax.broadcasted_iota(jnp.int32, (8 * DEPTH, 1), 0) % DEPTH
    kind = row - 9 * jnp.minimum(row // 9, 2)
    first = (kind == 0) | (kind == 3) | (kind == 5)
    second = (kind == 1) | (kind == 4)
    third = kind == 2
    constant = jnp.where((kind >= 6) & (kind < 9), 1.0, 0.0)
    for block in range(patches // 8):
        rows = [centred[block * 8 + k : block * 8 + k + 1, :] * own for k in range(8)]
        points = -2.0 * jnp.dot(
            jnp.concatenate(rows, axis=0), table, precision=HIGHEST, preferred_element_type=F32
        )
        rest = points - points.astype(BF16).astype(F32)
        last = rest - rest.astype(BF16).astype(F32)
        value = jnp.where(
            first, points, jnp.where(second, rest, jnp.where(third, last, constant))
        )
        features_ref[block * 8 * DEPTH : (block + 1) * 8 * DEPTH, :] = value.astype(BF16)


def own_features(ctrl, table):
    patches = ctrl.shape[1]
    return pl.pallas_call(
        own_features_kernel,
        out_shape=(
            jax.ShapeDtypeStruct((patches * DEPTH, CHILDREN), BF16),
            jax.ShapeDtypeStruct((patches, 128), F32),
            jax.ShapeDtypeStruct((patches, CHILDREN), F32),
        ),
        in_specs=[IN_VMEM] * 2,
        out_specs=(IN_VMEM,) * 3,
        compiler_params=pltpu.CompilerParams(vmem_limit_bytes=VMEM_BYTES),
        cost_estimate=pl.CostEstimate(
            flops=2_000_000_000, bytes_accessed=4_000_000, transcendentals=0
        ),
        name="own_features",
    )(ctrl, table)


def fill(number, place_ref, local_ref, value_ref, ctrl_ref, rows_ref, out_ref):
    patches = ctrl_ref.shape[1]
    rows_ref[:, :48] = ctrl_ref[...].T
    out_ref[...] = jnp.zeros(out_ref.shape, F32)
    lane = lax.broadcasted_iota(jnp.int32, (8, 128), 1)
    sub = lax.broadcasted_iota(jnp.int32, (8, 128), 0)
    c = lane % 4
    source = jnp.where(c == 3, 0, c * 16 + lane // 64 * 8 + sub)
    slot = lane % 64 // 4

    def body(step, carry):
        for u in range(GROUP):
            e = step * GROUP + u
            on = e < number
            place = jnp.where(on, place_ref[e], 0)
            local = jnp.where(on, local_ref[e], 0)
            here = jnp.where(on, place & (ROOM - 1), ROOM)
            row = jnp.broadcast_to(rows_ref[pl.ds(local, 1), :], (8, 128))
            moved = jnp.take_along_axis(row, source, axis=1, mode="promise_in_bounds")
            if value_ref is not None:
                label = jnp.where(on, value_ref[e], 0) + 1
                moved = jnp.where(c == 3, label.astype(F32), moved)
            block = place >> 4
            out_ref[block] = jnp.where(slot == here, moved, out_ref[block])
        return carry

    lax.fori_loop(0, (number + GROUP - 1) // GROUP, body, 0)


def offer_kernel(
    count_ref, a_ref, owner_ref, slot_ref, ctrl_ref, out_ref, place_ref, local_ref, rows_ref, used_ref
):
    number = count_ref[0]
    for o in range(used_ref.shape[0]):
        used_ref[o] = 0

    def rank(step, carry):
        for u in range(GROUP):
            e = step * GROUP + u
            owner = owner_ref[e]
            standing = used_ref[owner]
            used_ref[owner] = standing + 1
            place_ref[e] = owner * ROOM + standing
            local_ref[e] = a_ref[e]
        return carry

    lax.fori_loop(0, (number + GROUP - 1) // GROUP, rank, 0)
    fill(number, place_ref, local_ref, slot_ref, ctrl_ref, rows_ref, out_ref)


def offer(count, a, owner, slot, ctrl, devices):
    slots = a.shape[0]
    return pl.pallas_call(
        offer_kernel,
        out_shape=(
            jax.ShapeDtypeStruct((devices, 8, 128), F32),
            jax.ShapeDtypeStruct((slots + 32,), jnp.int32),
            jax.ShapeDtypeStruct((slots + 32,), jnp.int32),
        ),
        in_specs=[IN_SMEM] * 4 + [IN_VMEM],
        out_specs=(IN_VMEM, IN_SMEM, IN_SMEM),
        scratch_shapes=[
            pltpu.VMEM((ctrl.shape[1], 128), F32),
            pltpu.SMEM((devices,), jnp.int32),
        ],
        name="offer",
    )(count, a, owner, slot, ctrl)


def answer_kernel(label_ref, ctrl_ref, out_ref, number_ref, place_ref, local_ref, rows_ref):
    def listing(block, number):
        for j in range(ROOM):
            e = block * ROOM + j
            label = label_ref[e]
            place_ref[number] = e
            local_ref[number] = label - 1
            number = number + jnp.where(label > 0, 1, 0)
        return number

    number = lax.fori_loop(0, out_ref.shape[0], listing, 0)
    number_ref[0] = number
    fill(number, place_ref, local_ref, None, ctrl_ref, rows_ref, out_ref)


def answer(label, ctrl, devices):
    size = devices * ROOM + 32
    return pl.pallas_call(
        answer_kernel,
        out_shape=(
            jax.ShapeDtypeStruct((devices, 8, 128), F32),
            jax.ShapeDtypeStruct((1,), jnp.int32),
            jax.ShapeDtypeStruct((size,), jnp.int32),
            jax.ShapeDtypeStruct((size,), jnp.int32),
        ),
        in_specs=[IN_SMEM, IN_VMEM],
        out_specs=(IN_VMEM, IN_SMEM, IN_SMEM, IN_SMEM),
        scratch_shapes=[pltpu.VMEM((ctrl.shape[1], 128), F32)],
        name="answer",
    )(label, ctrl)


def nearest_kernel(
    number_ref,
    place_ref,
    local_ref,
    remote_ref,
    features_ref,
    centre_ref,
    norm_ref,
    table_ref,
    out_ref,
    least_ref,
    weight_ref,
    even_ref,
    odd_ref,
):
    patches = out_ref.shape[0]
    number = number_ref[0]
    least_ref[...] = jnp.full(least_ref.shape, 1e30, F32)
    weight_ref[...] = jnp.zeros(weight_ref.shape, BF16)
    lane = lax.broadcasted_iota(jnp.int32, (8, 128), 1)
    coordinate = jnp.minimum(lane % DEPTH // 9, 2)
    quarter = lane // DEPTH
    kind = (lane % DEPTH - 9 * coordinate)[:1]
    square = kind >= 6
    first = (kind <= 2) | (kind == 6)
    second = (kind == 3) | (kind == 4) | (kind == 7)
    table = table_ref[...]

    def entry(e):
        on = e < number
        local = jnp.where(on, local_ref[e], 0)
        return jnp.where(on, place_ref[e], 0), local, jnp.where(on, local, patches)

    def prepare(group, tile_ref):
        low = high = None
        for u in range(GROUP):
            place, local, _ = entry(group * GROUP + u)
            block = remote_ref[place >> 4]
            index = coordinate + 4 * (place & (ROOM - 1))
            centre = centre_ref[pl.ds(local, 1), :]
            one = jnp.take_along_axis(block, index, axis=1, mode="promise_in_bounds") - centre
            two = jnp.take_along_axis(block, index + 64, axis=1, mode="promise_in_bounds") - centre
            low = one if u == 0 else jnp.where(quarter == u, one, low)
            high = two if u == 0 else jnp.where(quarter == u, two, high)
        one, two, three = pieces(jnp.concatenate([low, high], axis=0))
        control = jnp.concatenate([one, one, one, two, two, three], axis=0)
        points = jnp.dot(table, control, preferred_element_type=F32)
        value = jnp.where(square, points * points, points)
        rest = value - value.astype(BF16).astype(F32)
        last = rest - rest.astype(BF16).astype(F32)
        tile_ref[...] = jnp.where(first, value, jnp.where(second, rest, last)).astype(BF16)

    def distances(group, tile_ref, half):
        for u in range(GROUP):
            _, local, row = entry(group * GROUP + u)
            weight_ref[half, u, DEPTH * u : DEPTH * (u + 1), :] = features_ref[
                pl.ds(pl.multiple_of(local * DEPTH, DEPTH), DEPTH), :
            ]
            apart = jnp.dot(tile_ref[...], weight_ref[half, u], preferred_element_type=F32)
            nearest = jnp.min(apart.reshape(CHILDREN // 8, 8, CHILDREN), axis=0)
            least_ref[row] = jnp.minimum(least_ref[row], nearest)

    prepare(0, even_ref)

    def body(step, carry):
        prepare(2 * step + 1, odd_ref)
        distances(2 * step, even_ref, 0)
        prepare(2 * step + 2, even_ref)
        distances(2 * step + 1, odd_ref, 1)
        return carry

    lax.fori_loop(0, (number + 2 * GROUP - 1) // (2 * GROUP), body, 0)
    nearest = jnp.min(least_ref[:patches], axis=1)
    out_ref[...] = jnp.clip(nearest + norm_ref[...], 0.0, CLIP_SQUARED)


def nearest(number, place, local, remote, own, table, name):
    features, centre, norm = own
    patches = norm.shape[0]
    return pl.pallas_call(
        nearest_kernel,
        out_shape=jax.ShapeDtypeStruct((patches, CHILDREN), F32),
        in_specs=[IN_SMEM] * 3 + [IN_VMEM] * 5,
        out_specs=IN_VMEM,
        scratch_shapes=[
            pltpu.VMEM((patches + 8, 8, CHILDREN), F32),
            pltpu.VMEM((2, GROUP, GROUP * DEPTH, CHILDREN), BF16),
            pltpu.VMEM((CHILDREN, GROUP * DEPTH), BF16),
            pltpu.VMEM((CHILDREN, GROUP * DEPTH), BF16),
        ],
        compiler_params=pltpu.CompilerParams(vmem_limit_bytes=VMEM_BYTES),
        cost_estimate=pl.CostEstimate(
            flops=20_000_000_000, bytes_accessed=4_000_000, transcendentals=0
        ),
        name=name,
    )(number, place, local, remote, features, centre, norm, table)


def on_device(ctrl_a, ctrl_b, pair_a, pair_b_owner, pair_b_slot, pair_count):
    devices = lax.axis_size("dev")
    table = jnp.asarray(bernstein_table().astype(np.float32))
    table_t = jnp.asarray(table_pieces())
    offered, place_a, local_a = offer(
        pair_count, pair_a, pair_b_owner[:, 0], pair_b_slot, ctrl_a, devices
    )
    asked = lax.all_to_all(offered, "dev", 0, 0, tiled=True)
    own_a = own_features(ctrl_a, table)
    own_b = own_features(ctrl_b, table)
    label = asked[:, 0, 3:64:4].astype(jnp.int32).reshape(-1)
    answered, number_b, place_b, local_b = answer(label, ctrl_b, devices)
    given = lax.all_to_all(answered, "dev", 0, 0, tiled=True)
    near_b = nearest(number_b, place_b, local_b, asked, own_b, table_t, "near_b")
    near_a = nearest(pair_count, place_a, local_a, given, own_a, table_t, "near_a")
    return (near_a, near_b)


def solution(mesh):
    in_specs = (
        P(None, ("grp", "dev")),
        P(None, ("grp", "dev")),
        P(("grp", "dev")),
        P(("grp", "dev"), None),
        P(("grp", "dev")),
        P(("grp", "dev")),
    )
    out_specs = (P(("grp", "dev"), None), P(("grp", "dev"), None))
    return jax.shard_map(
        on_device, mesh=mesh, in_specs=in_specs, out_specs=out_specs, check_vma=False
    )
```

```python
import jax
import jax.numpy as jnp
import ml_dtypes
import numpy as np
from jax import lax
from jax.experimental import pallas as pl
from jax.experimental.pallas import tpu as pltpu
from jax.sharding import PartitionSpec as P

SUB = 16
CHILDREN = SUB * SUB
CLIP_SQUARED = 4.0
ROOM = 16
GROUP = 4
DEPTH = 32
PLACES = 2048
VMEM_BYTES = 16 * 2**20
F32 = jnp.float32
BF16 = jnp.bfloat16
HIGHEST = lax.Precision.HIGHEST
IN_VMEM = pl.BlockSpec(memory_space=pltpu.VMEM)
IN_SMEM = pl.BlockSpec(memory_space=pltpu.SMEM)


def bernstein_table():
    along = (np.arange(SUB) + 0.5) / SUB
    other = 1.0 - along
    basis = np.stack([other**3, 3.0 * along * other**2, 3.0 * along**2 * other, along**3])
    return (basis[:, None, :, None] * basis[None, :, None, :]).reshape(16, CHILDREN)


def table_pieces():
    left = bernstein_table().T
    parts = []
    for _ in range(3):
        parts.append(left.astype(np.float32).astype(ml_dtypes.bfloat16))
        left = left - parts[-1].astype(np.float64)
    one, two, three = parts
    return np.concatenate([one, two, three, one, two, one], axis=1)


def pieces(x):
    one = x.astype(BF16)
    rest = x - one.astype(F32)
    two = rest.astype(BF16)
    return one, two, (rest - two.astype(F32)).astype(BF16)


def feature_kinds(shape, axis):
    f = lax.broadcasted_iota(jnp.int32, shape, axis) % DEPTH
    inner = f < 24
    return f, jnp.where(inner, f // 8, jnp.minimum(f - 24, 2)), jnp.where(inner, f % 8, 8)


def own_features_kernel(ctrl_ref, table_ref, features_ref, centre_ref, norm_ref, plane_ref):
    patches = ctrl_ref.shape[1]
    control = ctrl_ref[...].T
    table = table_ref[...]
    norm = jnp.zeros((patches, CHILDREN), F32)
    _, coordinate, _ = feature_kinds((1, 128), 1)
    centre = None
    for c in range(3):
        block = control[:, c * 16 : (c + 1) * 16]
        mean = jnp.sum(block, axis=1, keepdims=True) * (1.0 / 16.0)
        points = jnp.dot(block - mean, table, precision=HIGHEST, preferred_element_type=F32)
        norm = norm + points * points
        centre = mean if c == 0 else jnp.where(coordinate == c, mean, centre)
        points = -2.0 * points
        one = points.astype(BF16).astype(F32)
        rest = points - one
        two = rest.astype(BF16).astype(F32)
        plane_ref[3 * c] = one
        plane_ref[3 * c + 1] = two
        plane_ref[3 * c + 2] = rest - two
    norm_ref[...] = norm
    centre_ref[...] = centre
    row = lax.broadcasted_iota(jnp.int32, (8, CHILDREN), 0)
    first = (row == 0) | (row == 3) | (row == 5)
    second = (row == 1) | (row == 4)
    third = row == 2
    last = jnp.where(row < 3, 1.0, 0.0)

    def body(step, carry):
        for u in range(8):
            patch = step * 8 + u
            tiles = []
            for c in range(3):
                one, two, three = (
                    jnp.broadcast_to(plane_ref[3 * c + k, pl.ds(patch, 1), :], (8, CHILDREN))
                    for k in range(3)
                )
                tiles.append(
                    jnp.where(first, one, jnp.where(second, two, jnp.where(third, three, 1.0)))
                )
            features_ref[pl.ds(pl.multiple_of(patch * DEPTH, DEPTH), DEPTH), :] = jnp.concatenate(
                tiles + [last], axis=0
            ).astype(BF16)
        return carry

    lax.fori_loop(0, patches // 8, body, 0)


def own_features(ctrl, table):
    patches = ctrl.shape[1]
    return pl.pallas_call(
        own_features_kernel,
        out_shape=(
            jax.ShapeDtypeStruct((patches * DEPTH, CHILDREN), BF16),
            jax.ShapeDtypeStruct((patches, 128), F32),
            jax.ShapeDtypeStruct((patches, CHILDREN), F32),
        ),
        in_specs=[IN_VMEM] * 2,
        out_specs=(IN_VMEM,) * 3,
        scratch_shapes=[pltpu.VMEM((9, patches, CHILDREN), F32)],
        compiler_params=pltpu.CompilerParams(vmem_limit_bytes=VMEM_BYTES),
        cost_estimate=pl.CostEstimate(
            flops=2_000_000_000, bytes_accessed=4_000_000, transcendentals=0
        ),
        name="own_features",
    )(ctrl, table)


def spread_rows(ctrl_ref, rows_ref, spread_ref):
    rows_ref[:, :48] = ctrl_ref[...].T
    lane = lax.broadcasted_iota(jnp.int32, (8, 128), 1)
    sub = lax.broadcasted_iota(jnp.int32, (8, 128), 0)
    c = lane % 4
    source = jnp.where(c == 3, 0, c * 16 + lane // 64 * 8 + sub)

    def body(step, carry):
        for u in range(8):
            patch = step * 8 + u
            row = jnp.broadcast_to(rows_ref[pl.ds(patch, 1), :], (8, 128))
            spread_ref[patch] = jnp.take_along_axis(row, source, axis=1, mode="promise_in_bounds")
        return carry

    lax.fori_loop(0, spread_ref.shape[0] // 8, body, 0)
    return lane % 64 // 4, c == 3


def offer_kernel(count_ref, place_ref, code_ref, ctrl_ref, out_ref, rows_ref, spread_ref, held_ref):
    number = count_ref[0]
    devices = out_ref.shape[0]
    slot, labelled = spread_rows(ctrl_ref, rows_ref, spread_ref)

    def clear(step, carry):
        for u in range(32):
            held_ref[step * 32 + u] = 0
        return carry

    lax.fori_loop(0, devices * ROOM // 32, clear, 0)

    def hold(step, carry):
        for u in range(8):
            held_ref[place_ref[step * 8 + u]] = code_ref[step * 8 + u]
        return carry

    lax.fori_loop(0, (number + 7) // 8, hold, 0)

    def body(block, carry):
        value = jnp.zeros((8, 128), F32)
        for j in range(ROOM):
            code = held_ref[block * ROOM + j]
            row = jnp.where(labelled, (code >> 8).astype(F32), spread_ref[code & 127])
            value = jnp.where(slot == j, row, value)
        out_ref[block] = value
        return carry

    lax.fori_loop(0, devices, body, 0)


def offer(count, place, code, ctrl, devices):
    patches = ctrl.shape[1]
    return pl.pallas_call(
        offer_kernel,
        out_shape=jax.ShapeDtypeStruct((devices, 8, 128), F32),
        in_specs=[IN_SMEM] * 3 + [IN_VMEM],
        out_specs=IN_VMEM,
        scratch_shapes=[
            pltpu.VMEM((patches, 128), F32),
            pltpu.VMEM((patches, 8, 128), F32),
            pltpu.SMEM((devices * ROOM + 8,), jnp.int32),
        ],
        compiler_params=pltpu.CompilerParams(vmem_limit_bytes=VMEM_BYTES),
        name="offer",
    )(count, place, code, ctrl)


def answer_kernel(
    asked_ref, ctrl_ref, out_ref, number_ref, list_ref, rows_ref, spread_ref, code_ref, held_ref, sem
):
    devices = out_ref.shape[0]
    label = asked_ref[:, 0, :].astype(jnp.int32)
    lane = lax.broadcasted_iota(jnp.int32, label.shape, 1)
    block = lax.broadcasted_iota(jnp.int32, label.shape, 0)
    code_ref[...] = label * PLACES + block * ROOM + lane // 4
    copy = pltpu.make_async_copy(code_ref, held_ref, sem)
    copy.start()
    slot, _ = spread_rows(ctrl_ref, rows_ref, spread_ref)
    copy.wait()

    def body(block, number):
        value = jnp.zeros((8, 128), F32)
        for j in range(ROOM):
            code = held_ref[block, 4 * j + 3]
            list_ref[number] = code
            number = number + jnp.where(code >= PLACES, 1, 0)
            value = jnp.where(slot == j, spread_ref[jnp.maximum(code // PLACES - 1, 0)], value)
        out_ref[block] = value
        return number

    number_ref[0] = lax.fori_loop(0, devices, body, 0)


def answer(asked, ctrl, devices):
    patches = ctrl.shape[1]
    return pl.pallas_call(
        answer_kernel,
        out_shape=(
            jax.ShapeDtypeStruct((devices, 8, 128), F32),
            jax.ShapeDtypeStruct((1,), jnp.int32),
            jax.ShapeDtypeStruct((devices * ROOM + 32,), jnp.int32),
        ),
        in_specs=[IN_VMEM] * 2,
        out_specs=(IN_VMEM, IN_SMEM, IN_SMEM),
        scratch_shapes=[
            pltpu.VMEM((patches, 128), F32),
            pltpu.VMEM((patches, 8, 128), F32),
            pltpu.VMEM((devices, 128), jnp.int32),
            pltpu.SMEM((devices, 128), jnp.int32),
            pltpu.SemaphoreType.DMA,
        ],
        compiler_params=pltpu.CompilerParams(vmem_limit_bytes=VMEM_BYTES),
        name="answer",
    )(asked, ctrl)


def nearest_kernel(
    number_ref,
    list_ref,
    remote_ref,
    features_ref,
    centre_ref,
    norm_ref,
    table_ref,
    out_ref,
    least_ref,
    weight_ref,
    even_ref,
    odd_ref,
):
    patches = out_ref.shape[0]
    number = number_ref[0]
    least_ref[...] = jnp.full(least_ref.shape, 1e30, F32)
    weight_ref[...] = jnp.zeros(weight_ref.shape, BF16)
    _, coordinate, kind = feature_kinds((8, 128), 1)
    quarter = lax.broadcasted_iota(jnp.int32, (8, 128), 1) // DEPTH
    kind = kind[:1]
    square = kind >= 6
    first = (kind <= 2) | (kind == 6)
    second = (kind == 3) | (kind == 4) | (kind == 7)
    table = table_ref[...]

    def entry(e):
        on = e < number
        code = jnp.where(on, list_ref[jnp.minimum(e, list_ref.shape[0] - 1)], PLACES)
        local = code // PLACES - 1
        return code & (PLACES - 1), local, jnp.where(on, local, patches)

    def prepare(group, tile_ref):
        low = high = None
        for u in range(GROUP):
            place, local, _ = entry(group * GROUP + u)
            block = remote_ref[place >> 4]
            index = coordinate + 4 * (place & (ROOM - 1))
            centre = centre_ref[pl.ds(local, 1), :]
            one = jnp.take_along_axis(block, index, axis=1, mode="promise_in_bounds") - centre
            two = jnp.take_along_axis(block, index + 64, axis=1, mode="promise_in_bounds") - centre
            low = one if u == 0 else jnp.where(quarter == u, one, low)
            high = two if u == 0 else jnp.where(quarter == u, two, high)
        one, two, three = pieces(jnp.concatenate([low, high], axis=0))
        control = jnp.concatenate([one, one, one, two, two, three], axis=0)
        points = jnp.dot(table, control, preferred_element_type=F32)
        value = jnp.where(square, points * points, points)
        rest = value - value.astype(BF16).astype(F32)
        last = rest - rest.astype(BF16).astype(F32)
        tile_ref[...] = jnp.where(first, value, jnp.where(second, rest, last)).astype(BF16)

    def distances(group, tile_ref, half):
        for u in range(GROUP):
            _, local, row = entry(group * GROUP + u)
            weight_ref[half, u, DEPTH * u : DEPTH * (u + 1), :] = features_ref[
                pl.ds(pl.multiple_of(local * DEPTH, DEPTH), DEPTH), :
            ]
            apart = jnp.dot(tile_ref[...], weight_ref[half, u], preferred_element_type=F32)
            nearest = jnp.min(apart.reshape(CHILDREN // 8, 8, CHILDREN), axis=0)
            least_ref[row] = jnp.minimum(least_ref[row], nearest)

    prepare(0, even_ref)

    def body(step, carry):
        prepare(2 * step + 1, odd_ref)
        distances(2 * step, even_ref, 0)
        prepare(2 * step + 2, even_ref)
        distances(2 * step + 1, odd_ref, 1)
        return carry

    lax.fori_loop(0, (number + 2 * GROUP - 1) // (2 * GROUP), body, 0)
    nearest = jnp.min(least_ref[:patches], axis=1)
    out_ref[...] = jnp.clip(nearest + norm_ref[...], 0.0, CLIP_SQUARED)


def nearest(number, pairs, remote, own, table, name):
    features, centre, norm = own
    patches = norm.shape[0]
    return pl.pallas_call(
        nearest_kernel,
        out_shape=jax.ShapeDtypeStruct((patches, CHILDREN), F32),
        in_specs=[IN_SMEM] * 2 + [IN_VMEM] * 5,
        out_specs=IN_VMEM,
        scratch_shapes=[
            pltpu.VMEM((patches + 8, 8, CHILDREN), F32),
            pltpu.VMEM((2, GROUP, GROUP * DEPTH, CHILDREN), BF16),
            pltpu.VMEM((CHILDREN, GROUP * DEPTH), BF16),
            pltpu.VMEM((CHILDREN, GROUP * DEPTH), BF16),
        ],
        compiler_params=pltpu.CompilerParams(vmem_limit_bytes=VMEM_BYTES),
        cost_estimate=pl.CostEstimate(
            flops=20_000_000_000, bytes_accessed=4_000_000, transcendentals=0
        ),
        name=name,
    )(number, pairs, remote, features, centre, norm, table)


def on_device(ctrl_a, ctrl_b, pair_a, pair_b_owner, pair_b_slot, pair_count):
    devices = lax.axis_size("dev")
    table = jnp.asarray(bernstein_table().astype(np.float32))
    table_t = jnp.asarray(table_pieces())
    owner = pair_b_owner[:, 0]
    index = jnp.arange(owner.shape[0])
    same = owner[:, None] == owner[None, :]
    rank = jnp.sum(same & (index[None, :] < index[:, None]), axis=1, dtype=jnp.int32)
    place = jnp.where(index < pair_count[0], owner * ROOM + rank, devices * ROOM)
    offered = offer(pair_count, place, pair_a + (pair_b_slot + 1) * 256, ctrl_a, devices)
    asked = lax.all_to_all(offered, "dev", 0, 0, tiled=True)
    own_b = own_features(ctrl_b, table)
    own_a = own_features(ctrl_a, table)
    answered, number_b, pairs_b = answer(asked, ctrl_b, devices)
    given = lax.all_to_all(answered, "dev", 0, 0, tiled=True)
    near_b = nearest(number_b, pairs_b, asked, own_b, table_t, "near_b")
    near_a = nearest(pair_count, (pair_a + 1) * PLACES + place, given, own_a, table_t, "near_a")
    return (near_a, near_b)


def solution(mesh):
    in_specs = (
        P(None, ("grp", "dev")),
        P(None, ("grp", "dev")),
        P(("grp", "dev")),
        P(("grp", "dev"), None),
        P(("grp", "dev")),
        P(("grp", "dev")),
    )
    out_specs = (P(("grp", "dev"), None), P(("grp", "dev"), None))
    return jax.shard_map(
        on_device, mesh=mesh, in_specs=in_specs, out_specs=out_specs, check_vma=False
    )
```

```python
import jax
import jax.numpy as jnp
import ml_dtypes
import numpy as np
from jax import lax
from jax.experimental import pallas as pl
from jax.experimental.pallas import tpu as pltpu
from jax.sharding import PartitionSpec as P

SUB = 16
CHILDREN = SUB * SUB
CLIP_SQUARED = 4.0
ROOM = 16
GROUP = 8
STRIPS = 8
STRIP = CHILDREN // STRIPS
SPLIT_AT = {1: (0, 1), 2: (2, 3), 3: (4, 5), 4: (6, 7)}
GATHER_AT = 6
AHEAD = 2
UNITS = 2
PARTS = 1
DEPTH = 32
BITS = 11
VMEM_BYTES = 16 * 2**20
F32 = jnp.float32
BF16 = jnp.bfloat16
HIGHEST = lax.Precision.HIGHEST
IN_VMEM = pl.BlockSpec(memory_space=pltpu.VMEM)
IN_SMEM = pl.BlockSpec(memory_space=pltpu.SMEM)


def bernstein_table():
    along = (np.arange(SUB) + 0.5) / SUB
    other = 1.0 - along
    basis = np.stack([other**3, 3.0 * along * other**2, 3.0 * along**2 * other, along**3])
    return (basis[:, None, :, None] * basis[None, :, None, :]).reshape(16, CHILDREN)


def table_pieces():
    left = bernstein_table().T
    parts = []
    for _ in range(3):
        parts.append(left.astype(np.float32).astype(ml_dtypes.bfloat16))
        left = left - parts[-1].astype(np.float64)
    one, two, three = parts
    zero = np.zeros((CHILDREN, CHILDREN - 96), ml_dtypes.bfloat16)
    return np.concatenate([one, two, three, one, two, one, zero], axis=1)


def pieces(x):
    one = x.astype(BF16)
    rest = x - one.astype(F32)
    two = rest.astype(BF16)
    return one, two, (rest - two.astype(F32)).astype(BF16)


def feature_kinds(shape, axis):
    f = lax.broadcasted_iota(jnp.int32, shape, axis) % DEPTH
    inner = f < 24
    return f, jnp.where(inner, f // 8, jnp.minimum(f - 24, 2)), jnp.where(inner, f % 8, 8)


def own_features_kernel(ctrl_ref, table_ref, features_ref, centre_ref, norm_ref, plane_ref):
    patches = ctrl_ref.shape[1]
    control = ctrl_ref[...].T
    table = table_ref[...]
    norm = jnp.zeros((patches, CHILDREN), F32)
    _, coordinate, _ = feature_kinds((1, 128), 1)
    centre = None
    for c in range(3):
        block = control[:, c * 16 : (c + 1) * 16]
        mean = jnp.sum(block, axis=1, keepdims=True) * (1.0 / 16.0)
        points = jnp.dot(block - mean, table, precision=HIGHEST, preferred_element_type=F32)
        norm = norm + points * points
        centre = mean if c == 0 else jnp.where(coordinate == c, mean, centre)
        points = -2.0 * points
        one = points.astype(BF16).astype(F32)
        rest = points - one
        two = rest.astype(BF16).astype(F32)
        plane_ref[3 * c] = one
        plane_ref[3 * c + 1] = two
        plane_ref[3 * c + 2] = rest - two
    norm_ref[...] = norm
    centre_ref[...] = centre
    row = lax.broadcasted_iota(jnp.int32, (8, CHILDREN), 0)
    first = (row == 0) | (row == 3) | (row == 5)
    second = (row == 1) | (row == 4)
    third = row == 2
    last = jnp.where(row < 3, 1.0, 0.0)

    def body(step, carry):
        for u in range(8):
            patch = step * 8 + u
            tiles = []
            for c in range(3):
                one, two, three = (
                    jnp.broadcast_to(plane_ref[3 * c + k, pl.ds(patch, 1), :], (8, CHILDREN))
                    for k in range(3)
                )
                tiles.append(
                    jnp.where(first, one, jnp.where(second, two, jnp.where(third, three, 1.0)))
                )
            features_ref[pl.ds(pl.multiple_of(patch * DEPTH, DEPTH), DEPTH), :] = jnp.concatenate(
                tiles + [last], axis=0
            ).astype(BF16)
        return carry

    lax.fori_loop(0, patches // 8, body, 0)


def own_features(ctrl, table):
    patches = ctrl.shape[1]
    return pl.pallas_call(
        own_features_kernel,
        out_shape=(
            jax.ShapeDtypeStruct((patches * DEPTH, CHILDREN), BF16),
            jax.ShapeDtypeStruct((patches, 128), F32),
            jax.ShapeDtypeStruct((patches, CHILDREN), F32),
        ),
        in_specs=[IN_VMEM] * 2,
        out_specs=(IN_VMEM,) * 3,
        scratch_shapes=[pltpu.VMEM((9, patches, CHILDREN), F32)],
        compiler_params=pltpu.CompilerParams(vmem_limit_bytes=VMEM_BYTES),
        cost_estimate=pl.CostEstimate(
            flops=2_000_000_000, bytes_accessed=4_000_000, transcendentals=0
        ),
        name="own_features",
    )(ctrl, table)


def spread_rows(ctrl_ref, rows_ref, spread_ref):
    rows_ref[:, :48] = ctrl_ref[...].T
    lane = lax.broadcasted_iota(jnp.int32, (8, 128), 1)
    sub = lax.broadcasted_iota(jnp.int32, (8, 128), 0)
    c = lane % 4
    source = jnp.where(c == 3, 0, c * 16 + lane // 64 * 8 + sub)

    def body(step, carry):
        for u in range(8):
            patch = step * 8 + u
            row = jnp.broadcast_to(rows_ref[pl.ds(patch, 1), :], (8, 128))
            spread_ref[patch] = jnp.take_along_axis(row, source, axis=1, mode="promise_in_bounds")
        return carry

    lax.fori_loop(0, spread_ref.shape[0] // 8, body, 0)
    return lane % 64 // 4, c == 3


def offer_kernel(count_ref, place_ref, code_ref, ctrl_ref, out_ref, rows_ref, spread_ref, held_ref):
    number = count_ref[0]
    devices = out_ref.shape[0]
    slot, labelled = spread_rows(ctrl_ref, rows_ref, spread_ref)

    def clear(step, carry):
        for u in range(32):
            held_ref[step * 32 + u] = 0
        return carry

    lax.fori_loop(0, devices * ROOM // 32, clear, 0)

    def hold(step, carry):
        entries = [(place_ref[step * 8 + u], code_ref[step * 8 + u]) for u in range(8)]
        for place, code in entries:
            held_ref[place] = code
        return carry

    lax.fori_loop(0, (number + 7) // 8, hold, 0)

    def body(block, carry):
        codes = [held_ref[block * ROOM + j] for j in range(ROOM)]
        value = jnp.zeros((8, 128), F32)
        label = jnp.zeros((8, 128), jnp.int32)
        for j, code in enumerate(codes):
            value = jnp.where(slot == j, spread_ref[code & 255], value)
            label = jnp.where(slot == j, code >> 8, label)
        out_ref[block] = jnp.where(labelled, label.astype(F32), value)
        return carry

    lax.fori_loop(0, devices, body, 0)


def offer(count, place, code, ctrl, devices):
    patches = ctrl.shape[1]
    return pl.pallas_call(
        offer_kernel,
        out_shape=jax.ShapeDtypeStruct((devices, 8, 128), F32),
        in_specs=[IN_SMEM] * 3 + [IN_VMEM],
        out_specs=IN_VMEM,
        scratch_shapes=[
            pltpu.VMEM((patches, 128), F32),
            pltpu.VMEM((patches, 8, 128), F32),
            pltpu.SMEM((devices * ROOM + 8,), jnp.int32),
        ],
        compiler_params=pltpu.CompilerParams(vmem_limit_bytes=VMEM_BYTES),
        name="offer",
    )(count, place, code, ctrl)


def answer_kernel(
    asked_ref, ctrl_ref, out_ref, number_ref, list_ref, rows_ref, spread_ref, code_ref, held_ref, sem
):
    devices = out_ref.shape[0]
    label = asked_ref[:, 0, :].astype(jnp.int32)
    lane = lax.broadcasted_iota(jnp.int32, label.shape, 1)
    block = lax.broadcasted_iota(jnp.int32, label.shape, 0)
    used = jnp.where((lane < 64) & (lane % 4 == 3) & (label > 0), 1, 0)
    used = jnp.sum(used.astype(F32), axis=1, keepdims=True).astype(jnp.int32)
    code_ref[...] = jnp.where(lane == 0, used, label * (1 << BITS) + block * ROOM + lane // 4)
    copy = pltpu.make_async_copy(code_ref, held_ref, sem)
    copy.start()
    slot, _ = spread_rows(ctrl_ref, rows_ref, spread_ref)
    copy.wait()

    def body(block, number):
        codes = [held_ref[block, 4 * j + 3] for j in range(ROOM)]
        used = held_ref[block, 0]
        value = jnp.zeros((8, 128), F32)
        for j, code in enumerate(codes):
            patch = jnp.maximum((code >> BITS) - 1, 0)
            value = jnp.where(slot == j, spread_ref[patch], value)
        out_ref[block] = value
        for j, code in enumerate(codes):
            list_ref[number + j] = code
        return number + used

    number_ref[0] = lax.fori_loop(0, devices, body, 0)


def answer(asked, ctrl, devices):
    patches = ctrl.shape[1]
    return pl.pallas_call(
        answer_kernel,
        out_shape=(
            jax.ShapeDtypeStruct((devices, 8, 128), F32),
            jax.ShapeDtypeStruct((1,), jnp.int32),
            jax.ShapeDtypeStruct((devices * ROOM + 32,), jnp.int32),
        ),
        in_specs=[IN_VMEM] * 2,
        out_specs=(IN_VMEM, IN_SMEM, IN_SMEM),
        scratch_shapes=[
            pltpu.VMEM((patches, 128), F32),
            pltpu.VMEM((patches, 8, 128), F32),
            pltpu.VMEM((devices, 128), jnp.int32),
            pltpu.SMEM((devices, 128), jnp.int32),
            pltpu.SemaphoreType.DMA,
        ],
        compiler_params=pltpu.CompilerParams(vmem_limit_bytes=VMEM_BYTES),
        name="answer",
    )(asked, ctrl)


def nearest_kernel(
    number_ref,
    list_ref,
    remote_ref,
    features_ref,
    centre_ref,
    norm_ref,
    table_ref,
    out_ref,
    least_ref,
    weight_ref,
    even_ref,
    odd_ref,
    control_ref,
):
    patches = out_ref.shape[0]
    number = number_ref[0]
    least_ref[...] = jnp.full(least_ref.shape, 1e30, F32)
    weight_ref[...] = jnp.zeros(weight_ref.shape, BF16)
    _, coordinate, kind = feature_kinds((8, 128), 1)
    quarter = lax.broadcasted_iota(jnp.int32, (8, 128), 1) // DEPTH
    kind = jnp.concatenate([kind[:1]] * 2, axis=1)
    square = kind >= 6
    first = (kind <= 2) | (kind == 6)
    second = (kind == 3) | (kind == 4) | (kind == 7)
    def entry(e):
        on = e < number
        code = jnp.where(on, list_ref[jnp.minimum(e, list_ref.shape[0] - 1)], 1 << BITS)
        local = (code >> BITS) - 1
        return code & ((1 << BITS) - 1), local, jnp.where(on, local, patches)

    def run(*units):
        point_refs = (units[:STRIPS], units[STRIPS : 2 * STRIPS])
        units = units[2 * STRIPS :]
        apart_refs = [
            [units[(m * UNITS + k) * PARTS : (m * UNITS + k + 1) * PARTS] for k in range(UNITS)]
            for m in range(2)
        ]

        def gather(group, half):
            strips = []
            for side in range(GROUP // 4):
                low = high = None
                for u in range(4):
                    place, local, _ = entry(group * GROUP + 4 * side + u)
                    block = remote_ref[place >> 4]
                    index = coordinate + 4 * (place & (ROOM - 1))
                    centre = centre_ref[pl.ds(local, 1), :]
                    one = jnp.take_along_axis(block, index, axis=1, mode="promise_in_bounds")
                    two = jnp.take_along_axis(block, index + 64, axis=1, mode="promise_in_bounds")
                    one, two = one - centre, two - centre
                    low = one if u == 0 else jnp.where(quarter == u, one, low)
                    high = two if u == 0 else jnp.where(quarter == u, two, high)
                one, two, three = pieces(jnp.concatenate([low, high], axis=0))
                strips.append(jnp.concatenate([one, one, one, two, two, three], axis=0))
            control_ref[half, :96, :] = jnp.concatenate(strips, axis=1)

        def evaluate(half):
            pltpu.matmul_push_rhs(control_ref[half], 0, half)
            for k, point_ref in enumerate(point_refs[half]):
                pltpu.matmul_acc_lhs(
                    point_ref,
                    table_ref[STRIP * k : STRIP * (k + 1), :],
                    load_staged_rhs=0 if k == 0 else None,
                )

        def split(half, k):
            points = pltpu.matmul_pop(point_refs[half][k])
            value = jnp.where(square, points * points, points)
            rest = value - value.astype(BF16).astype(F32)
            last = rest - rest.astype(BF16).astype(F32)
            tiles[1 - half][STRIP * k : STRIP * (k + 1), :] = jnp.where(
                first, value, jnp.where(second, rest, last)
            ).astype(BF16)

        def start(group, half, u):
            _, local, _ = entry(group * GROUP + u)
            weight_ref[half, u, DEPTH * u : DEPTH * (u + 1), :] = features_ref[
                pl.ds(pl.multiple_of(local * DEPTH, DEPTH), DEPTH), :
            ]
            unit, stage = u % 2, u // 2 % 2
            pltpu.matmul_push_rhs(weight_ref[half, u], stage, unit)
            rows = CHILDREN // PARTS
            turn = (half * GROUP + u) // 2 % UNITS
            for k, apart_ref in enumerate(apart_refs[unit][turn]):
                pltpu.matmul_acc_lhs(
                    apart_ref,
                    tiles[half][rows * k : rows * (k + 1), :],
                    load_staged_rhs=stage if k == 0 else None,
                )

        def finish(group, half, u):
            nearest = None
            for apart_ref in apart_refs[u % 2][(half * GROUP + u) // 2 % UNITS]:
                apart = pltpu.matmul_pop(apart_ref)
                part = jnp.min(apart.reshape(-1, 8, CHILDREN), axis=0)
                nearest = part if nearest is None else jnp.minimum(nearest, part)
            _, _, row = entry(group * GROUP + u)
            least_ref[row] = jnp.minimum(least_ref[row], nearest)

        tiles = (even_ref, odd_ref)
        control_ref[...] = jnp.zeros(control_ref.shape, BF16)
        gather(0, 1)
        evaluate(1)
        gather(1, 0)
        for k in range(STRIPS):
            split(1, k)
        for u in range(AHEAD):
            start(0, 0, u)

        def body(step, carry):
            for half in range(2):
                group = 2 * step + half
                evaluate(half)
                for u in range(GROUP):
                    if u in SPLIT_AT:
                        for k in SPLIT_AT[u]:
                            split(half, k)
                    if u + AHEAD < GROUP:
                        start(group, half, u + AHEAD)
                    else:
                        start(group + 1, 1 - half, u + AHEAD - GROUP)
                    finish(group, half, u)
                    if u == GATHER_AT:
                        gather(group + 2, 1 - half)
            return carry

        steps = (number + 2 * GROUP - 1) // (2 * GROUP)
        lax.fori_loop(0, steps, body, 0)
        for u in range(AHEAD):
            finish(2 * steps, 0, u)

    pl.run_scoped(
        run,
        *(pltpu.ACC(m)((STRIP, CHILDREN), F32) for m in range(2) for _ in range(STRIPS)),
        *(
            pltpu.ACC(m)((CHILDREN // PARTS, CHILDREN), F32)
            for m in range(2)
            for _ in range(UNITS * PARTS)
        ),
    )
    nearest = jnp.min(least_ref[:patches], axis=1)
    out_ref[...] = jnp.clip(nearest + norm_ref[...], 0.0, CLIP_SQUARED)


def nearest(number, pairs, remote, own, table, name):
    features, centre, norm = own
    patches = norm.shape[0]
    return pl.pallas_call(
        nearest_kernel,
        out_shape=jax.ShapeDtypeStruct((patches, CHILDREN), F32),
        in_specs=[IN_SMEM] * 2 + [IN_VMEM] * 5,
        out_specs=IN_VMEM,
        scratch_shapes=[
            pltpu.VMEM((patches + 8, 8, CHILDREN), F32),
            pltpu.VMEM((2, GROUP, GROUP * DEPTH, CHILDREN), BF16),
            pltpu.VMEM((CHILDREN, GROUP * DEPTH), BF16),
            pltpu.VMEM((CHILDREN, GROUP * DEPTH), BF16),
            pltpu.VMEM((2, CHILDREN, CHILDREN), BF16),
        ],
        compiler_params=pltpu.CompilerParams(vmem_limit_bytes=VMEM_BYTES),
        cost_estimate=pl.CostEstimate(
            flops=20_000_000_000, bytes_accessed=4_000_000, transcendentals=0
        ),
        name=name,
    )(number, pairs, remote, features, centre, norm, table)


def on_device(ctrl_a, ctrl_b, pair_a, pair_b_owner, pair_b_slot, pair_count):
    devices = lax.axis_size("dev")
    table = jnp.asarray(bernstein_table().astype(np.float32))
    table_t = jnp.asarray(table_pieces())
    owner = pair_b_owner[:, 0]
    index = jnp.arange(owner.shape[0])
    same = owner[:, None] == owner[None, :]
    rank = jnp.sum(same & (index[None, :] < index[:, None]), axis=1, dtype=jnp.int32)
    place = jnp.where(index < pair_count[0], owner * ROOM + rank, devices * ROOM)
    offered = offer(pair_count, place, pair_a + (pair_b_slot + 1) * 256, ctrl_a, devices)
    asked = lax.all_to_all(offered, "dev", 0, 0, tiled=True)
    own_b = own_features(ctrl_b, table)
    own_a = own_features(ctrl_a, table)
    answered, number_b, pairs_b = answer(asked, ctrl_b, devices)
    given = lax.all_to_all(answered, "dev", 0, 0, tiled=True)
    near_b = nearest(number_b, pairs_b, asked, own_b, table_t, "near_b")
    near_a = nearest(pair_count, ((pair_a + 1) << BITS) + place, given, own_a, table_t, "near_a")
    return (near_a, near_b)


def solution(mesh):
    in_specs = (
        P(None, ("grp", "dev")),
        P(None, ("grp", "dev")),
        P(("grp", "dev")),
        P(("grp", "dev"), None),
        P(("grp", "dev")),
        P(("grp", "dev")),
    )
    out_specs = (P(("grp", "dev"), None), P(("grp", "dev"), None))
    return jax.shard_map(
        on_device, mesh=mesh, in_specs=in_specs, out_specs=out_specs, check_vma=False
    )
```

```python
import jax
import jax.numpy as jnp
import ml_dtypes
import numpy as np
from jax import lax
from jax.experimental import pallas as pl
from jax.experimental.pallas import tpu as pltpu
from jax.sharding import PartitionSpec as P

SUB = 16
CHILDREN = SUB * SUB
CLIP_SQUARED = 4.0
ROOM = 16
GROUP = 8
SIDE = 4
STRIPS = 8
STRIP = CHILDREN // STRIPS
SPLIT_AT = {(1, 0): (0,1), (1, 1): (2,), (2, 0): (3,4), (2, 1): (5,), (3, 0): (6,7)}
PARTS = 2
ROWS = CHILDREN // PARTS
UNITS = 2
DEPTH = 32
BITS = 11
VMEM_BYTES = 16 * 2**20
F32 = jnp.float32
BF16 = jnp.bfloat16
HIGHEST = lax.Precision.HIGHEST
IN_VMEM = pl.BlockSpec(memory_space=pltpu.VMEM)
IN_SMEM = pl.BlockSpec(memory_space=pltpu.SMEM)


def bernstein_table():
    along = (np.arange(SUB) + 0.5) / SUB
    other = 1.0 - along
    basis = np.stack([other**3, 3.0 * along * other**2, 3.0 * along**2 * other, along**3])
    return (basis[:, None, :, None] * basis[None, :, None, :]).reshape(16, CHILDREN)


def table_pieces():
    left = bernstein_table().T
    parts = []
    for _ in range(3):
        parts.append(left.astype(np.float32).astype(ml_dtypes.bfloat16))
        left = left - parts[-1].astype(np.float64)
    one, two, three = parts
    zero = np.zeros((CHILDREN, CHILDREN - 96), ml_dtypes.bfloat16)
    return np.concatenate([one, two, three, one, two, one, zero], axis=1)


def pieces(x):
    one = x.astype(BF16)
    rest = x - one.astype(F32)
    two = rest.astype(BF16)
    return one, two, (rest - two.astype(F32)).astype(BF16)


def feature_kinds(shape, axis):
    f = lax.broadcasted_iota(jnp.int32, shape, axis) % DEPTH
    inner = f < 24
    return f, jnp.where(inner, f // 8, jnp.minimum(f - 24, 2)), jnp.where(inner, f % 8, 8)


def own_features_kernel(ctrl_ref, table_ref, features_ref, centre_ref, norm_ref, plane_ref):
    patches = ctrl_ref.shape[1]
    control = ctrl_ref[...].T
    table = table_ref[...]
    norm = jnp.zeros((patches, CHILDREN), F32)
    _, coordinate, _ = feature_kinds((1, 128), 1)
    centre = None
    for c in range(3):
        block = control[:, c * 16 : (c + 1) * 16]
        mean = jnp.sum(block, axis=1, keepdims=True) * (1.0 / 16.0)
        points = jnp.dot(block - mean, table, precision=HIGHEST, preferred_element_type=F32)
        norm = norm + points * points
        centre = mean if c == 0 else jnp.where(coordinate == c, mean, centre)
        points = -2.0 * points
        one = points.astype(BF16).astype(F32)
        rest = points - one
        two = rest.astype(BF16).astype(F32)
        plane_ref[3 * c] = one
        plane_ref[3 * c + 1] = two
        plane_ref[3 * c + 2] = rest - two
    norm_ref[...] = norm
    centre_ref[...] = centre
    row = lax.broadcasted_iota(jnp.int32, (8, CHILDREN), 0)
    first = (row == 0) | (row == 3) | (row == 5)
    second = (row == 1) | (row == 4)
    third = row == 2
    last = jnp.where(row < 3, 1.0, 0.0)

    def body(step, carry):
        for u in range(8):
            patch = step * 8 + u
            tiles = []
            for c in range(3):
                one, two, three = (
                    jnp.broadcast_to(plane_ref[3 * c + k, pl.ds(patch, 1), :], (8, CHILDREN))
                    for k in range(3)
                )
                tiles.append(
                    jnp.where(first, one, jnp.where(second, two, jnp.where(third, three, 1.0)))
                )
            features_ref[pl.ds(pl.multiple_of(patch * DEPTH, DEPTH), DEPTH), :] = jnp.concatenate(
                tiles + [last], axis=0
            ).astype(BF16)
        return carry

    lax.fori_loop(0, patches // 8, body, 0)


def own_features(ctrl, table):
    patches = ctrl.shape[1]
    return pl.pallas_call(
        own_features_kernel,
        out_shape=(
            jax.ShapeDtypeStruct((patches * DEPTH, CHILDREN), BF16),
            jax.ShapeDtypeStruct((patches, 128), F32),
            jax.ShapeDtypeStruct((patches, CHILDREN), F32),
        ),
        in_specs=[IN_VMEM] * 2,
        out_specs=(IN_VMEM,) * 3,
        scratch_shapes=[pltpu.VMEM((9, patches, CHILDREN), F32)],
        compiler_params=pltpu.CompilerParams(vmem_limit_bytes=VMEM_BYTES),
        cost_estimate=pl.CostEstimate(
            flops=2_000_000_000, bytes_accessed=4_000_000, transcendentals=0
        ),
        name="own_features",
    )(ctrl, table)


def spread_rows(ctrl_ref, rows_ref, spread_ref):
    rows_ref[:, :48] = ctrl_ref[...].T
    lane = lax.broadcasted_iota(jnp.int32, (8, 128), 1)
    sub = lax.broadcasted_iota(jnp.int32, (8, 128), 0)
    c = lane % 4
    source = jnp.where(c == 3, 0, c * 16 + lane // 64 * 8 + sub)

    def body(step, carry):
        for u in range(32):
            patch = step * 32 + u
            row = jnp.broadcast_to(rows_ref[pl.ds(patch, 1), :], (8, 128))
            spread_ref[patch] = jnp.take_along_axis(row, source, axis=1, mode="promise_in_bounds")
        return carry

    lax.fori_loop(0, spread_ref.shape[0] // 32, body, 0)
    return lane % 64 // 4, c == 3


def offer_kernel(count_ref, place_ref, code_ref, ctrl_ref, out_ref, rows_ref, spread_ref):
    number = count_ref[0]
    devices = out_ref.shape[0]
    slot, labelled = spread_rows(ctrl_ref, rows_ref, spread_ref)

    out_ref[...] = jnp.zeros(out_ref.shape, F32)

    def body(step, carry):
        entries = [(place_ref[step * 8 + u], code_ref[step * 8 + u]) for u in range(8)]
        for place, code in entries:
            row = jnp.where(labelled, (code >> 8).astype(F32), spread_ref[code & 127])
            block = jnp.minimum(place >> 4, devices - 1)
            here = slot == jnp.where(place < devices * ROOM, place & (ROOM - 1), ROOM)
            pltpu.store(out_ref.at[block], row, mask=here)
        return carry

    lax.fori_loop(0, (number + 7) // 8, body, 0)


def offer(count, place, code, ctrl, devices):
    patches = ctrl.shape[1]
    return pl.pallas_call(
        offer_kernel,
        out_shape=jax.ShapeDtypeStruct((devices, 8, 128), F32),
        in_specs=[IN_SMEM] * 3 + [IN_VMEM],
        out_specs=IN_VMEM,
        scratch_shapes=[
            pltpu.VMEM((patches, 128), F32),
            pltpu.VMEM((patches, 8, 128), F32),
        ],
        compiler_params=pltpu.CompilerParams(vmem_limit_bytes=VMEM_BYTES),
        name="offer",
    )(count, place, code, ctrl)


def answer_kernel(
    asked_ref, ctrl_ref, out_ref, number_ref, list_ref, rows_ref, spread_ref, code_ref, held_ref, sem
):
    devices = out_ref.shape[0]
    label = asked_ref[:, 0, :].astype(jnp.int32)
    lane = lax.broadcasted_iota(jnp.int32, label.shape, 1)
    block = lax.broadcasted_iota(jnp.int32, label.shape, 0)
    used = jnp.where((lane < 64) & (lane % 4 == 3) & (label > 0), 1, 0)
    used = jnp.sum(used.astype(F32), axis=1, keepdims=True).astype(jnp.int32)
    code_ref[...] = jnp.where(lane == 0, used, label * (1 << BITS) + block * ROOM + lane // 4)
    copy = pltpu.make_async_copy(code_ref, held_ref, sem)
    copy.start()
    slot, _ = spread_rows(ctrl_ref, rows_ref, spread_ref)
    copy.wait()

    def body(step, carry):
        for block in [step * SIDE + k for k in range(SIDE)]:
            codes = [held_ref[block, 4 * j + 3] for j in range(ROOM)]
            value = jnp.zeros((8, 128), F32)
            for j, code in enumerate(codes):
                patch = jnp.maximum((code >> BITS) - 1, 0)
                value = jnp.where(slot == j, spread_ref[patch], value)
            out_ref[block] = value
        return carry

    lax.fori_loop(0, devices // SIDE, body, 0)

    def listing(block, number):
        codes = [held_ref[block, 4 * j + 3] for j in range(ROOM)]
        used = held_ref[block, 0]
        for j, code in enumerate(codes):
            list_ref[number + j] = code
        return number + used

    number_ref[0] = lax.fori_loop(0, devices, listing, 0)


def answer(asked, ctrl, devices):
    patches = ctrl.shape[1]
    return pl.pallas_call(
        answer_kernel,
        out_shape=(
            jax.ShapeDtypeStruct((devices, 8, 128), F32),
            jax.ShapeDtypeStruct((1,), jnp.int32),
            jax.ShapeDtypeStruct((devices * ROOM + 32,), jnp.int32),
        ),
        in_specs=[IN_VMEM] * 2,
        out_specs=(IN_VMEM, IN_SMEM, IN_SMEM),
        scratch_shapes=[
            pltpu.VMEM((patches, 128), F32),
            pltpu.VMEM((patches, 8, 128), F32),
            pltpu.VMEM((devices, 128), jnp.int32),
            pltpu.SMEM((devices, 128), jnp.int32),
            pltpu.SemaphoreType.DMA,
        ],
        compiler_params=pltpu.CompilerParams(vmem_limit_bytes=VMEM_BYTES),
        name="answer",
    )(asked, ctrl)


def nearest_kernel(
    number_ref,
    list_ref,
    remote_ref,
    features_ref,
    centre_ref,
    norm_ref,
    table_ref,
    out_ref,
    least_ref,
    weight_ref,
    even_ref,
    odd_ref,
    control_ref,
):
    patches = out_ref.shape[0]
    number = number_ref[0]
    least_ref[...] = jnp.full(least_ref.shape, 1e30, F32)
    _, coordinate, kind = feature_kinds((8, 128), 1)
    quarter = lax.broadcasted_iota(jnp.int32, (8, 128), 1) // DEPTH
    kind = jnp.concatenate([kind[:1]] * 2, axis=1)
    square = kind >= 6
    first = (kind <= 2) | (kind == 6)
    second = (kind == 3) | (kind == 4) | (kind == 7)
    def entry(e):
        on = e < number
        code = jnp.where(on, list_ref[jnp.minimum(e, list_ref.shape[0] - 1)], 1 << BITS)
        local = (code >> BITS) - 1
        return code & ((1 << BITS) - 1), local, jnp.where(on, local, patches)

    def run(*units):
        point_refs = (units[:STRIPS], units[STRIPS : 2 * STRIPS])
        units = units[2 * STRIPS :]
        apart_refs = [
            [units[(m * UNITS + k) * PARTS : (m * UNITS + k + 1) * PARTS] for k in range(UNITS)]
            for m in range(2)
        ]

        def gather(group, half):
            strips = []
            for side in range(GROUP // 4):
                low = high = None
                for u in range(4):
                    place, local, _ = entry(group * GROUP + 4 * side + u)
                    block = remote_ref[place >> 4]
                    index = coordinate + 4 * (place & (ROOM - 1))
                    centre = centre_ref[pl.ds(local, 1), :]
                    one = jnp.take_along_axis(block, index, axis=1, mode="promise_in_bounds")
                    two = jnp.take_along_axis(block, index + 64, axis=1, mode="promise_in_bounds")
                    one, two = one - centre, two - centre
                    low = one if u == 0 else jnp.where(quarter == u, one, low)
                    high = two if u == 0 else jnp.where(quarter == u, two, high)
                one, two, three = pieces(jnp.concatenate([low, high], axis=0))
                strips.append(jnp.concatenate([one, one, one, two, two, three], axis=0))
            control_ref[half, :96, :] = jnp.concatenate(strips, axis=1)

        def evaluate(half):
            pltpu.matmul_push_rhs(control_ref[half], 0, half)
            for k, point_ref in enumerate(point_refs[half]):
                pltpu.matmul_acc_lhs(
                    point_ref,
                    table_ref[STRIP * k : STRIP * (k + 1), :],
                    load_staged_rhs=0 if k == 0 else None,
                )

        def split(half, k):
            points = pltpu.matmul_pop(point_refs[half][k])
            value = jnp.where(square, points * points, points)
            rest = value - value.astype(BF16).astype(F32)
            last = rest - rest.astype(BF16).astype(F32)
            tiles[1 - half][STRIP * k : STRIP * (k + 1), :] = jnp.where(
                first, value, jnp.where(second, rest, last)
            ).astype(BF16)

        def weigh(group, half):
            for u in range(GROUP):
                _, local, _ = entry(group * GROUP + u)
                weight_ref[half, DEPTH * u : DEPTH * (u + 1), :] = features_ref[
                    pl.ds(pl.multiple_of(local * DEPTH, DEPTH), DEPTH), :
                ]

        def load(group, half, v):
            if v == 0:
                for m in range(2):
                    pltpu.matmul_push_rhs(weight_ref[half], 1, m)

        def rows_of(half, u, k):
            side = u // 4 * 128
            rows = slice(ROWS * k, ROWS * (k + 1))
            part = tiles[half][rows, side : side + 128] * only[u % 4]
            zero = jnp.zeros((ROWS, 128), BF16)
            return jnp.concatenate([zero, part] if side else [part, zero], axis=1)

        def couple(group, half, v, first):
            load(group, half, v)
            nearest = [None, None]
            for k in range(PARTS):
                for m in range(2):
                    pltpu.matmul_acc_lhs(
                        apart_refs[m][v % 2][k],
                        rows_of(half, 2 * v + m, k),
                        load_staged_rhs=1 if k == 0 and v == 0 else None,
                    )
                if not first:
                    take(v - 1, k, nearest)
                for strip in SPLIT_AT.get((v, k), ()):
                    split(half, strip)
            if not first:
                keep(group * GROUP + 2 * v - 2, nearest)

        def take(v, k, nearest):
            for m in range(2):
                apart = pltpu.matmul_pop(apart_refs[m][v % 2][k])
                part = jnp.min(apart.reshape(-1, 8, CHILDREN), axis=0)
                nearest[m] = part if k == 0 else jnp.minimum(nearest[m], part)

        def keep(e, nearest):
            for m in range(2):
                _, _, row = entry(e + m)
                least_ref[row] = jnp.minimum(least_ref[row], nearest[m])

        tiles = (even_ref, odd_ref)
        lane = lax.broadcasted_iota(jnp.int32, (16, 128), 1) // DEPTH
        only = [jnp.where(lane == u, 1.0, 0.0).astype(BF16)[:1] for u in range(4)]
        control_ref[...] = jnp.zeros(control_ref.shape, BF16)
        gather(0, 1)
        evaluate(1)
        gather(1, 0)
        for k in range(STRIPS):
            split(1, k)
        weigh(0, 0)
        weigh(1, 1)
        evaluate(0)
        couple(0, 0, 0, True)

        def body(step, carry):
            for half in range(2):
                group = 2 * step + half
                for v in range(1, GROUP // 2):
                    couple(group, half, v, False)
                    if v == 1:
                        gather(group + 2, 1 - half)
                weigh(group + 2, half)
                evaluate(1 - half)
                couple(group + 1, 1 - half, 0, False)
            return carry

        steps = (number + 2 * GROUP - 1) // (2 * GROUP)
        lax.fori_loop(0, steps, body, 0)
        for k in range(PARTS):
            take(0, k, [None, None] if k == 0 else [jnp.zeros((8, CHILDREN), F32)] * 2)
        for k in range(STRIPS):
            pltpu.matmul_pop(point_refs[0][k])

    pl.run_scoped(
        run,
        *(pltpu.ACC(m)((STRIP, CHILDREN), F32) for m in range(2) for _ in range(STRIPS)),
        *(
            pltpu.ACC(m)((CHILDREN // PARTS, CHILDREN), F32)
            for m in range(2)
            for _ in range(UNITS * PARTS)
        ),
    )
    nearest = jnp.min(least_ref[:patches], axis=1)
    out_ref[...] = jnp.clip(nearest + norm_ref[...], 0.0, CLIP_SQUARED)


def nearest(number, pairs, remote, own, table, name):
    features, centre, norm = own
    patches = norm.shape[0]
    return pl.pallas_call(
        nearest_kernel,
        out_shape=jax.ShapeDtypeStruct((patches, CHILDREN), F32),
        in_specs=[IN_SMEM] * 2 + [IN_VMEM] * 5,
        out_specs=IN_VMEM,
        scratch_shapes=[
            pltpu.VMEM((patches + 8, 8, CHILDREN), F32),
            pltpu.VMEM((2, GROUP * DEPTH, CHILDREN), BF16),
            pltpu.VMEM((CHILDREN, GROUP * DEPTH), BF16),
            pltpu.VMEM((CHILDREN, GROUP * DEPTH), BF16),
            pltpu.VMEM((2, CHILDREN, CHILDREN), BF16),
        ],
        compiler_params=pltpu.CompilerParams(vmem_limit_bytes=VMEM_BYTES),
        cost_estimate=pl.CostEstimate(
            flops=20_000_000_000, bytes_accessed=4_000_000, transcendentals=0
        ),
        name=name,
    )(number, pairs, remote, features, centre, norm, table)


def on_device(ctrl_a, ctrl_b, pair_a, pair_b_owner, pair_b_slot, pair_count):
    devices = lax.axis_size("dev")
    table = jnp.asarray(bernstein_table().astype(np.float32))
    table_t = jnp.asarray(table_pieces())
    owner = pair_b_owner[:, 0]
    index = jnp.arange(owner.shape[0])
    same = owner[:, None] == owner[None, :]
    rank = jnp.sum(same & (index[None, :] < index[:, None]), axis=1, dtype=jnp.int32)
    place = jnp.where(index < pair_count[0], owner * ROOM + rank, devices * ROOM)
    offered = offer(pair_count, place, pair_a + (pair_b_slot + 1) * 256, ctrl_a, devices)
    asked = lax.all_to_all(offered, "dev", 0, 0, tiled=True)
    own_b = own_features(ctrl_b, table)
    own_a = own_features(ctrl_a, table)
    answered, number_b, pairs_b = answer(asked, ctrl_b, devices)
    given = lax.all_to_all(answered, "dev", 0, 0, tiled=True)
    near_b = nearest(number_b, pairs_b, asked, own_b, table_t, "near_b")
    near_a = nearest(pair_count, ((pair_a + 1) << BITS) + place, given, own_a, table_t, "near_a")
    return (near_a, near_b)


def solution(mesh):
    in_specs = (
        P(None, ("grp", "dev")),
        P(None, ("grp", "dev")),
        P(("grp", "dev")),
        P(("grp", "dev"), None),
        P(("grp", "dev")),
        P(("grp", "dev")),
    )
    out_specs = (P(("grp", "dev"), None), P(("grp", "dev"), None))
    return jax.shard_map(
        on_device, mesh=mesh, in_specs=in_specs, out_specs=out_specs, check_vma=False
    )
```

```python
import jax
import jax.numpy as jnp
import ml_dtypes
import numpy as np
from jax import lax
from jax.experimental import pallas as pl
from jax.experimental.pallas import tpu as pltpu
from jax.sharding import PartitionSpec as P

SUB = 16
CHILDREN = SUB * SUB
CLIP_SQUARED = 4.0
ROOM = 16
GROUP = 8
SIDE = 4
STRIPS = 8
STRIP = CHILDREN // STRIPS
SPLIT_AT = {(1, 0): (0,1), (1, 1): (2,), (2, 0): (3,4), (2, 1): (5,), (3, 0): (6,7)}
PARTS = 2
ROWS = CHILDREN // PARTS
UNITS = 2
DEPTH = 32
BITS = 11
VMEM_BYTES = 16 * 2**20
F32 = jnp.float32
BF16 = jnp.bfloat16
HIGHEST = lax.Precision.HIGHEST
IN_VMEM = pl.BlockSpec(memory_space=pltpu.VMEM)
IN_SMEM = pl.BlockSpec(memory_space=pltpu.SMEM)


def bernstein_table():
    along = (np.arange(SUB) + 0.5) / SUB
    other = 1.0 - along
    basis = np.stack([other**3, 3.0 * along * other**2, 3.0 * along**2 * other, along**3])
    return (basis[:, None, :, None] * basis[None, :, None, :]).reshape(16, CHILDREN)


def table_pieces():
    left = bernstein_table().T
    parts = []
    for _ in range(3):
        parts.append(left.astype(np.float32).astype(ml_dtypes.bfloat16))
        left = left - parts[-1].astype(np.float64)
    one, two, three = parts
    zero = np.zeros((CHILDREN, CHILDREN - 96), ml_dtypes.bfloat16)
    return np.concatenate([one, two, three, one, two, one, zero], axis=1)


def pieces(x):
    one = x.astype(BF16)
    rest = x - one.astype(F32)
    two = rest.astype(BF16)
    return one, two, (rest - two.astype(F32)).astype(BF16)


def feature_kinds(shape, axis):
    f = lax.broadcasted_iota(jnp.int32, shape, axis) % DEPTH
    inner = f < 24
    return f, jnp.where(inner, f // 8, jnp.minimum(f - 24, 2)), jnp.where(inner, f % 8, 8)


def own_features_kernel(ctrl_ref, table_ref, features_ref, centre_ref, norm_ref, plane_ref):
    patches = ctrl_ref.shape[1]
    control = ctrl_ref[...].T
    table = table_ref[...]
    norm = jnp.zeros((patches, CHILDREN), F32)
    _, coordinate, _ = feature_kinds((1, 128), 1)
    centre = None
    for c in range(3):
        block = control[:, c * 16 : (c + 1) * 16]
        mean = jnp.sum(block, axis=1, keepdims=True) * (1.0 / 16.0)
        points = jnp.dot(block - mean, table, precision=HIGHEST, preferred_element_type=F32)
        norm = norm + points * points
        centre = mean if c == 0 else jnp.where(coordinate == c, mean, centre)
        points = -2.0 * points
        one = points.astype(BF16).astype(F32)
        rest = points - one
        two = rest.astype(BF16).astype(F32)
        plane_ref[3 * c] = one
        plane_ref[3 * c + 1] = two
        plane_ref[3 * c + 2] = rest - two
    norm_ref[...] = norm
    centre_ref[...] = centre
    row = lax.broadcasted_iota(jnp.int32, (8, CHILDREN), 0)
    first = (row == 0) | (row == 3) | (row == 5)
    second = (row == 1) | (row == 4)
    third = row == 2
    last = jnp.where(row < 3, 1.0, 0.0)

    def body(step, carry):
        for u in range(8):
            patch = step * 8 + u
            tiles = []
            for c in range(3):
                one, two, three = (
                    jnp.broadcast_to(plane_ref[3 * c + k, pl.ds(patch, 1), :], (8, CHILDREN))
                    for k in range(3)
                )
                tiles.append(
                    jnp.where(first, one, jnp.where(second, two, jnp.where(third, three, 1.0)))
                )
            features_ref[pl.ds(pl.multiple_of(patch * DEPTH, DEPTH), DEPTH), :] = jnp.concatenate(
                tiles + [last], axis=0
            ).astype(BF16)
        return carry

    lax.fori_loop(0, patches // 8, body, 0)


def own_features(ctrl, table):
    patches = ctrl.shape[1]
    return pl.pallas_call(
        own_features_kernel,
        out_shape=(
            jax.ShapeDtypeStruct((patches * DEPTH, CHILDREN), BF16),
            jax.ShapeDtypeStruct((patches, 128), F32),
            jax.ShapeDtypeStruct((patches, CHILDREN), F32),
        ),
        in_specs=[IN_VMEM] * 2,
        out_specs=(IN_VMEM,) * 3,
        scratch_shapes=[pltpu.VMEM((9, patches, CHILDREN), F32)],
        compiler_params=pltpu.CompilerParams(vmem_limit_bytes=VMEM_BYTES),
        cost_estimate=pl.CostEstimate(
            flops=2_000_000_000, bytes_accessed=4_000_000, transcendentals=0
        ),
        name="own_features",
    )(ctrl, table)


def spread_rows(ctrl_ref, rows_ref, spread_ref):
    rows_ref[:, :48] = ctrl_ref[...].T
    lane = lax.broadcasted_iota(jnp.int32, (8, 128), 1)
    sub = lax.broadcasted_iota(jnp.int32, (8, 128), 0)
    c = lane % 4
    source = jnp.where(c == 3, 0, c * 16 + lane // 64 * 8 + sub)

    def body(step, carry):
        for u in range(32):
            patch = step * 32 + u
            row = jnp.broadcast_to(rows_ref[pl.ds(patch, 1), :], (8, 128))
            spread_ref[patch] = jnp.take_along_axis(row, source, axis=1, mode="promise_in_bounds")
        return carry

    lax.fori_loop(0, spread_ref.shape[0] // 32, body, 0)
    return lane % 64 // 4, c == 3


def offer_kernel(count_ref, place_ref, code_ref, ctrl_ref, out_ref, rows_ref, spread_ref):
    number = count_ref[0]
    devices = out_ref.shape[0]
    slot, labelled = spread_rows(ctrl_ref, rows_ref, spread_ref)

    out_ref[...] = jnp.zeros(out_ref.shape, F32)

    def body(step, carry):
        entries = [(place_ref[step * 8 + u], code_ref[step * 8 + u]) for u in range(8)]
        for place, code in entries:
            row = jnp.where(labelled, (code >> 8).astype(F32), spread_ref[code & 127])
            block = jnp.minimum(place >> 4, devices - 1)
            here = slot == jnp.where(place < devices * ROOM, place & (ROOM - 1), ROOM)
            pltpu.store(out_ref.at[block], row, mask=here)
        return carry

    lax.fori_loop(0, (number + 7) // 8, body, 0)


def offer(count, place, code, ctrl, devices):
    patches = ctrl.shape[1]
    return pl.pallas_call(
        offer_kernel,
        out_shape=jax.ShapeDtypeStruct((devices, 8, 128), F32),
        in_specs=[IN_SMEM] * 3 + [IN_VMEM],
        out_specs=IN_VMEM,
        scratch_shapes=[
            pltpu.VMEM((patches, 128), F32),
            pltpu.VMEM((patches, 8, 128), F32),
        ],
        compiler_params=pltpu.CompilerParams(vmem_limit_bytes=VMEM_BYTES),
        name="offer",
    )(count, place, code, ctrl)


def answer_kernel(
    asked_ref, ctrl_ref, out_ref, number_ref, list_ref, rows_ref, spread_ref, code_ref, held_ref, sem
):
    devices = out_ref.shape[0]
    label = asked_ref[:, 0, :].astype(jnp.int32)
    lane = lax.broadcasted_iota(jnp.int32, label.shape, 1)
    block = lax.broadcasted_iota(jnp.int32, label.shape, 0)
    used = jnp.where((lane < 64) & (lane % 4 == 3) & (label > 0), 1, 0)
    used = jnp.sum(used.astype(F32), axis=1, keepdims=True).astype(jnp.int32)
    patch = jnp.maximum(pltpu.roll(label, 127, axis=1) - 1, 0)
    code = jnp.where(lane % 4 == 3, label * (1 << BITS) + block * ROOM + lane // 4, patch)
    code_ref[...] = jnp.where(lane == 0, used, code)
    copy = pltpu.make_async_copy(code_ref, held_ref, sem)
    copy.start()
    slot, _ = spread_rows(ctrl_ref, rows_ref, spread_ref)
    copy.wait()

    def body(step, carry):
        for block in [step * SIDE + k for k in range(SIDE)]:
            patches = [held_ref[block, 4 * j + 2] for j in range(ROOM)]
            value = jnp.zeros((8, 128), F32)
            for j, patch in enumerate(patches):
                value = jnp.where(slot == j, spread_ref[patch], value)
            out_ref[block] = value
        return carry

    lax.fori_loop(0, devices // SIDE, body, 0)

    def listing(block, number):
        codes = [held_ref[block, 4 * j + 3] for j in range(ROOM)]
        used = held_ref[block, 0]
        for j, code in enumerate(codes):
            list_ref[number + j] = code
        return number + used

    number_ref[0] = lax.fori_loop(0, devices, listing, 0)


def answer(asked, ctrl, devices):
    patches = ctrl.shape[1]
    return pl.pallas_call(
        answer_kernel,
        out_shape=(
            jax.ShapeDtypeStruct((devices, 8, 128), F32),
            jax.ShapeDtypeStruct((1,), jnp.int32),
            jax.ShapeDtypeStruct((devices * ROOM + 32,), jnp.int32),
        ),
        in_specs=[IN_VMEM] * 2,
        out_specs=(IN_VMEM, IN_SMEM, IN_SMEM),
        scratch_shapes=[
            pltpu.VMEM((patches, 128), F32),
            pltpu.VMEM((patches, 8, 128), F32),
            pltpu.VMEM((devices, 128), jnp.int32),
            pltpu.SMEM((devices, 128), jnp.int32),
            pltpu.SemaphoreType.DMA,
        ],
        compiler_params=pltpu.CompilerParams(vmem_limit_bytes=VMEM_BYTES),
        name="answer",
    )(asked, ctrl)


def nearest_kernel(
    number_ref,
    list_ref,
    remote_ref,
    features_ref,
    centre_ref,
    norm_ref,
    table_ref,
    out_ref,
    least_ref,
    weight_ref,
    even_ref,
    odd_ref,
    control_ref,
):
    patches = out_ref.shape[0]
    number = number_ref[0]
    least_ref[...] = jnp.full(least_ref.shape, 1e30, F32)
    _, coordinate, kind = feature_kinds((8, 128), 1)
    quarter = lax.broadcasted_iota(jnp.int32, (8, 128), 1) // DEPTH
    kind = jnp.concatenate([kind[:1]] * 2, axis=1)
    square = kind >= 6
    first = (kind <= 2) | (kind == 6)
    second = (kind == 3) | (kind == 4) | (kind == 7)
    def entry(e):
        on = e < number
        code = jnp.where(on, list_ref[jnp.minimum(e, list_ref.shape[0] - 1)], 1 << BITS)
        local = (code >> BITS) - 1
        return code & ((1 << BITS) - 1), local, jnp.where(on, local, patches)

    def run(*units):
        point_refs = (units[:STRIPS], units[STRIPS : 2 * STRIPS])
        units = units[2 * STRIPS :]
        apart_refs = [
            [units[(m * UNITS + k) * PARTS : (m * UNITS + k + 1) * PARTS] for k in range(UNITS)]
            for m in range(2)
        ]

        def gather(group, half):
            strips = []
            for side in range(GROUP // 4):
                low = high = None
                for u in range(4):
                    place, local, _ = entry(group * GROUP + 4 * side + u)
                    block = remote_ref[place >> 4]
                    index = coordinate + 4 * (place & (ROOM - 1))
                    centre = centre_ref[pl.ds(local, 1), :]
                    one = jnp.take_along_axis(block, index, axis=1, mode="promise_in_bounds")
                    two = jnp.take_along_axis(block, index + 64, axis=1, mode="promise_in_bounds")
                    one, two = one - centre, two - centre
                    low = one if u == 0 else jnp.where(quarter == u, one, low)
                    high = two if u == 0 else jnp.where(quarter == u, two, high)
                one, two, three = pieces(jnp.concatenate([low, high], axis=0))
                strips.append(jnp.concatenate([one, one, one, two, two, three], axis=0))
            control_ref[half, :96, :] = jnp.concatenate(strips, axis=1)

        def evaluate(half):
            for m in range(2):
                pltpu.matmul_push_rhs(control_ref[half], 0, m)
            for k in range(STRIPS // 2):
                for m in range(2):
                    strip = m * STRIPS // 2 + k
                    pltpu.matmul_acc_lhs(
                        point_refs[half][strip],
                        table_ref[STRIP * strip : STRIP * (strip + 1), :],
                        load_staged_rhs=0 if k == 0 else None,
                    )

        def split(half, k):
            points = pltpu.matmul_pop(point_refs[half][k])
            value = jnp.where(square, points * points, points)
            rest = value - value.astype(BF16).astype(F32)
            last = rest - rest.astype(BF16).astype(F32)
            tiles[1 - half][STRIP * k : STRIP * (k + 1), :] = jnp.where(
                first, value, jnp.where(second, rest, last)
            ).astype(BF16)

        def weigh(group, half):
            for u in range(GROUP):
                _, local, _ = entry(group * GROUP + u)
                weight_ref[half, DEPTH * u : DEPTH * (u + 1), :] = features_ref[
                    pl.ds(pl.multiple_of(local * DEPTH, DEPTH), DEPTH), :
                ]

        def load(group, half, v):
            if v == 0:
                for m in range(2):
                    pltpu.matmul_push_rhs(weight_ref[half], 1, m)

        def rows_of(half, u, k):
            side = u // 4 * 128
            rows = slice(ROWS * k, ROWS * (k + 1))
            part = tiles[half][rows, side : side + 128] * only[u % 4]
            zero = jnp.zeros((ROWS, 128), BF16)
            return jnp.concatenate([zero, part] if side else [part, zero], axis=1)

        def couple(group, half, v, first):
            load(group, half, v)
            nearest = [None, None]
            for k in range(PARTS):
                for m in range(2):
                    pltpu.matmul_acc_lhs(
                        apart_refs[m][v % 2][k],
                        rows_of(half, 2 * v + m, k),
                        load_staged_rhs=1 if k == 0 and v == 0 else None,
                    )
                if not first:
                    take(v - 1, k, nearest)
                for strip in SPLIT_AT.get((v, k), ()):
                    split(half, strip)
            if not first:
                keep(group * GROUP + 2 * v - 2, nearest)

        def take(v, k, nearest):
            for m in range(2):
                apart = pltpu.matmul_pop(apart_refs[m][v % 2][k])
                part = jnp.min(apart.reshape(-1, 8, CHILDREN), axis=0)
                nearest[m] = part if k == 0 else jnp.minimum(nearest[m], part)

        def keep(e, nearest):
            for m in range(2):
                _, _, row = entry(e + m)
                least_ref[row] = jnp.minimum(least_ref[row], nearest[m])

        tiles = (even_ref, odd_ref)
        lane = lax.broadcasted_iota(jnp.int32, (16, 128), 1) // DEPTH
        only = [jnp.where(lane == u, 1.0, 0.0).astype(BF16)[:1] for u in range(4)]
        control_ref[...] = jnp.zeros(control_ref.shape, BF16)
        gather(0, 1)
        evaluate(1)
        gather(1, 0)
        for k in range(STRIPS):
            split(1, k)
        weigh(0, 0)
        weigh(1, 1)
        evaluate(0)
        couple(0, 0, 0, True)

        def body(step, carry):
            for half in range(2):
                group = 2 * step + half
                for v in range(1, GROUP // 2):
                    couple(group, half, v, False)
                    if v == 1:
                        gather(group + 2, 1 - half)
                weigh(group + 2, half)
                evaluate(1 - half)
                couple(group + 1, 1 - half, 0, False)
            return carry

        steps = (number + 2 * GROUP - 1) // (2 * GROUP)
        lax.fori_loop(0, steps, body, 0)
        for k in range(PARTS):
            take(0, k, [None, None] if k == 0 else [jnp.zeros((8, CHILDREN), F32)] * 2)
        for k in range(STRIPS):
            pltpu.matmul_pop(point_refs[0][k])

    pl.run_scoped(
        run,
        *(
            pltpu.ACC(k // (STRIPS // 2))((STRIP, CHILDREN), F32)
            for _ in range(2)
            for k in range(STRIPS)
        ),
        *(
            pltpu.ACC(m)((CHILDREN // PARTS, CHILDREN), F32)
            for m in range(2)
            for _ in range(UNITS * PARTS)
        ),
    )
    nearest = jnp.min(least_ref[:patches], axis=1)
    out_ref[...] = jnp.clip(nearest + norm_ref[...], 0.0, CLIP_SQUARED)


def nearest(number, pairs, remote, own, table, name):
    features, centre, norm = own
    patches = norm.shape[0]
    return pl.pallas_call(
        nearest_kernel,
        out_shape=jax.ShapeDtypeStruct((patches, CHILDREN), F32),
        in_specs=[IN_SMEM] * 2 + [IN_VMEM] * 5,
        out_specs=IN_VMEM,
        scratch_shapes=[
            pltpu.VMEM((patches + 8, 8, CHILDREN), F32),
            pltpu.VMEM((2, GROUP * DEPTH, CHILDREN), BF16),
            pltpu.VMEM((CHILDREN, GROUP * DEPTH), BF16),
            pltpu.VMEM((CHILDREN, GROUP * DEPTH), BF16),
            pltpu.VMEM((2, CHILDREN, CHILDREN), BF16),
        ],
        compiler_params=pltpu.CompilerParams(vmem_limit_bytes=VMEM_BYTES),
        cost_estimate=pl.CostEstimate(
            flops=20_000_000_000, bytes_accessed=4_000_000, transcendentals=0
        ),
        name=name,
    )(number, pairs, remote, features, centre, norm, table)


def on_device(ctrl_a, ctrl_b, pair_a, pair_b_owner, pair_b_slot, pair_count):
    devices = lax.axis_size("dev")
    table = jnp.asarray(bernstein_table().astype(np.float32))
    table_t = jnp.asarray(table_pieces())
    owner = pair_b_owner[:, 0]
    index = jnp.arange(owner.shape[0])
    same = owner[:, None] == owner[None, :]
    rank = jnp.sum(same & (index[None, :] < index[:, None]), axis=1, dtype=jnp.int32)
    place = jnp.where(index < pair_count[0], owner * ROOM + rank, devices * ROOM)
    offered = offer(pair_count, place, pair_a + (pair_b_slot + 1) * 256, ctrl_a, devices)
    asked = lax.all_to_all(offered, "dev", 0, 0, tiled=True)
    own_b = own_features(ctrl_b, table)
    own_a = own_features(ctrl_a, table)
    answered, number_b, pairs_b = answer(asked, ctrl_b, devices)
    given = lax.all_to_all(answered, "dev", 0, 0, tiled=True)
    near_b = nearest(number_b, pairs_b, asked, own_b, table_t, "near_b")
    near_a = nearest(pair_count, ((pair_a + 1) << BITS) + place, given, own_a, table_t, "near_a")
    return (near_a, near_b)


def solution(mesh):
    in_specs = (
        P(None, ("grp", "dev")),
        P(None, ("grp", "dev")),
        P(("grp", "dev")),
        P(("grp", "dev"), None),
        P(("grp", "dev")),
        P(("grp", "dev")),
    )
    out_specs = (P(("grp", "dev"), None), P(("grp", "dev"), None))
    return jax.shard_map(
        on_device, mesh=mesh, in_specs=in_specs, out_specs=out_specs, check_vma=False
    )
```
